32 devices in a mesh: inst: 8 (over y, x, core), mesh: 4 (over z).
Axes of the slice: x: 2, y: 2, z: 4, core: 2. Of those that a mesh axis runs over, the one named last changes fastest.
Arguments:
- state: float32 [16, 128, 5, 128], P('inst', 'mesh'), may hold values from -6 to 6
- cell_block: float32 [16, 128, 5, 5, 128], P('inst', 'mesh'), may hold values from -3 to 3
- face_block: float32 [16, 128, 6, 5, 5, 128], P('inst', 'mesh'), may hold values from -1.8 to 1.8
- neighbor: int32 [128, 6], P('mesh'), may hold values from 0 to 47
- face_cell: int32 [128, 6, 128], P('mesh'), may hold values from 0 to 127
- send_list: int32 [4, 2, 8], P('mesh'), may hold values from 0 to 31
- send_count: int32 [4, 2], P('mesh'), may hold values from 1 to 8, as said below
Outputs:
- product: float32 [16, 128, 5, 128], P('inst', 'mesh')
The draws below stay inside these ranges and needn't reach their ends.
Inputs may be any that keep to these rules, and one draw needn't show every extreme that they name: `send_count`: the first partition always sends 8 tiles to its lower neighbour.
All inputs are finite; a program needn't handle non-finite values.
Results may differ from the reference program's by a relative error of at most 0.0003.
Values sent between devices are 32-bit elements; how exact they have to be, the bound alone decides.
A program may use at most 128 MiB of HBM per device.

```python
import math
import jax
import jax.numpy as jnp
from jax import lax

INST = 16
NVAR = 5
TILE = 128
NB = 6
TILES_DEV = 32
HALO_MAX = 8
TILES = 128
N_MESH = 4


def draw_send_count(key, part):
    key = jax.random.fold_in(key, 7)
    counts = jax.random.randint(key, (N_MESH, 2), 1, HALO_MAX + 1)
    row_index = jnp.arange(N_MESH, dtype=jnp.int32)[:, None]
    col_index = jnp.arange(2, dtype=jnp.int32)[None, :]
    corner = (row_index == 0) & (col_index == 0)
    return jnp.where(corner, HALO_MAX, counts).astype(jnp.int32)


def plant(values, own_key, smallest, largest):
    place = [jax.random.randint(jax.random.fold_in(own_key, axis), (), 0, length) for axis, length in enumerate(values.shape)]
    main_axis = values.shape.index(max(values.shape))
    beside = place[:main_axis] + [(place[main_axis] + 1) % values.shape[main_axis]] + place[main_axis + 1:]
    return values.at[tuple(place)].set(smallest).at[tuple(beside)].set(largest)


def level_of(key, dims, pieces, smallest, top_value):
    def one(dim, blocks):
        draws = jax.random.uniform(jax.random.fold_in(jax.random.fold_in(key, 6), dim), (blocks,), jnp.float32, smallest / len(pieces), top_value / len(pieces))
        return jnp.repeat(jnp.exp(draws), dims[dim] // blocks).reshape((-1,) + (1,) * (len(dims) - dim - 1))

    factor_of = one(*pieces[0])
    for cut in pieces[1:]:
        factor_of = factor_of * one(*cut)
    return factor_of


def noise(stream_key, shape, deviation, limit, split=(), kind=jnp.bfloat16):
    drawn = jax.random.normal(stream_key, shape, jnp.float32) * deviation
    if len(split) > 0:
        drawn = level_of(stream_key, shape, split, -0.22, 0.18) * drawn
    return jnp.clip(drawn, min=-limit, max=limit).astype(kind)


def setup_inputs(seed: int = 0) -> dict:
    seeds = jax.random.split(jax.random.key(seed), 8)
    state = noise(seeds[0], (INST, TILES, NVAR, TILE), 1.0, 6.0, ((0, 8), (1, 4)), jnp.float32)
    cell_block = noise(seeds[1], (INST, TILES, NVAR, NVAR, TILE), 0.5, 3.0, ((0, 8), (1, 4)), jnp.float32)
    face_block = noise(seeds[2], (INST, TILES, NB, NVAR, NVAR, TILE), 0.3, 1.8, ((0, 8), (1, 4)), jnp.float32)
    neighbor = plant(jax.random.randint(seeds[3], (TILES, NB), 0, TILES_DEV + 2 * HALO_MAX), jax.random.fold_in(seeds[3], 1), 0, (TILES_DEV + 2 * HALO_MAX) - 1).astype(jnp.int32)
    face_cell = plant(jax.random.randint(seeds[4], (TILES, NB, TILE), 0, TILE), jax.random.fold_in(seeds[4], 1), 0, TILE - 1).astype(jnp.int32)
    send_list = plant(jax.random.randint(seeds[5], (N_MESH, 2, HALO_MAX), 0, TILES_DEV), jax.random.fold_in(seeds[5], 1), 0, TILES_DEV - 1).astype(jnp.int32)
    send_count = draw_send_count(jax.random.fold_in(seeds[7], 71), 0)
    return {"state": state, "cell_block": cell_block, "face_block": face_block, "neighbor": neighbor, "face_cell": face_cell, "send_list": send_list, "send_count": send_count}


DISSIPATION = 0.05


def spectral_matrix(count):
    row_index = jnp.arange(count, dtype=jnp.int32)[:, None]
    col_index = jnp.arange(count, dtype=jnp.int32)[None, :]
    offset = row_index - col_index
    angle = (math.pi / count) * offset.astype(jnp.float32)
    parity = (1 - 2 * (offset % 2)).astype(jnp.float32)
    sine_safe = jnp.where(offset == 0, jnp.float32(1.0), jnp.sin(angle))
    first_order = 0.5 * parity * jnp.cos(angle) / sine_safe
    second_order = -0.5 * parity / (sine_safe * sine_safe)
    values = first_order + DISSIPATION * second_order
    diagonal_value = jnp.float32(-DISSIPATION * (count * count + 2) / 12.0)
    return jnp.where(offset == 0, diagonal_value, values)


def fetch(buffer, slots, cells):
    inst_rows = buffer.shape[0]
    total_tiles = buffer.shape[1]
    flattened = jnp.transpose(buffer, (0, 2, 1, 3)).reshape(inst_rows, NVAR, total_tiles * TILE)
    indices = (slots[:, :, None] * TILE + cells).reshape(-1)
    facing = jnp.take(flattened, indices, axis=2)
    facing = facing.reshape(inst_rows, NVAR, slots.shape[0], slots.shape[1], TILE)
    return jnp.transpose(facing, (0, 2, 3, 1, 4))


def couple(blocks, facing):
    return jnp.sum(blocks * facing[:, :, :, None], axis=(2, 4))


def packet(part_state, listed, count_now):
    picked = jnp.take(part_state, listed, axis=1)
    active = jnp.arange(listed.shape[0], dtype=jnp.int32) < count_now
    return jnp.where(active[None, :, None, None], picked, 0.0)


def reference(state, cell_block, face_block, neighbor, face_cell, send_list, send_count):
    dmatrix = spectral_matrix(INST)
    spectral = jnp.einsum('nm,mtac->ntac', dmatrix, state, precision=lax.Precision.HIGHEST)
    cell_term = jnp.sum(cell_block * state[:, :, None], axis=3)
    slab_state = state.reshape(INST, N_MESH, TILES_DEV, NVAR, TILE)
    upward = jax.vmap(packet, in_axes=(1, 0, 0))(slab_state, send_list[:, 1], send_count[:, 1])
    downward = jax.vmap(packet, in_axes=(1, 0, 0))(slab_state, send_list[:, 0], send_count[:, 0])
    from_lower = jnp.roll(upward, 1, axis=0)
    from_upper = jnp.roll(downward, -1, axis=0)

    def one_part(partition):
        own_tiles = lax.dynamic_index_in_dim(slab_state, partition, 1, keepdims=False)
        lower = lax.dynamic_index_in_dim(from_lower, partition, 0, keepdims=False)
        upper = lax.dynamic_index_in_dim(from_upper, partition, 0, keepdims=False)
        buffer = jnp.concatenate([own_tiles, lower, upper], axis=1)
        first_tile = (partition * TILES_DEV).astype(jnp.int32)
        slots = lax.dynamic_slice_in_dim(neighbor, first_tile, TILES_DEV, 0)
        cells = lax.dynamic_slice_in_dim(face_cell, first_tile, TILES_DEV, 0)
        blocks = lax.dynamic_slice_in_dim(face_block, first_tile, TILES_DEV, 1)
        return couple(blocks, fetch(buffer, slots, cells))

    face_parts = lax.map(one_part, jnp.arange(N_MESH, dtype=jnp.int32))
    face_term = jnp.transpose(face_parts, (1, 0, 2, 3, 4)).reshape(INST, TILES, NVAR, TILE)
    return spectral + cell_term + face_term
```

```python
import functools
import math

import jax
import jax.numpy as jnp
from jax import lax
from jax.experimental import pallas as pl
from jax.experimental.pallas import tpu as pltpu
from jax.sharding import PartitionSpec as P

DISSIPATION = 0.05
LANES = 128
ROWS = 8
MESH = pl.DeviceIdType.MESH


def spectral_coefficient(offset, count):
    offset = offset % count
    if offset == 0:
        return -DISSIPATION * (count * count + 2) / 12.0
    angle = math.pi * offset / count
    parity = 1 - 2 * (offset % 2)
    sine = math.sin(angle)
    return 0.5 * parity * math.cos(angle) / sine - DISSIPATION * 0.5 * parity / (sine * sine)


def split(values):
    high = values.astype(jnp.bfloat16)
    rest = values - high.astype(jnp.float32)
    middle = rest.astype(jnp.bfloat16)
    low = (rest - middle.astype(jnp.float32)).astype(jnp.bfloat16)
    return high, middle, low


def kernel(
    groups, parts,
    state_hbm, cell_hbm, face_hbm, slot_hbm, index_hbm, list_hbm, count_hbm,
    out_ref,
    own, cell, face, slots, index, listed, counts,
    outgoing, incoming, solved, returned, packets, halo, table, facing, total,
    local_sem, face_sem, send_one, recv_one, send_two, recv_two, send_halo, recv_halo,
):
    inst, nvar, tiles = own.shape[0], own.shape[1], own.shape[2]
    nb = index.shape[0]
    most = listed.shape[1]
    share = tiles // groups
    count = inst * groups
    rows = inst * share
    me = lax.axis_index("inst")
    place = lax.axis_index("mesh")
    upper = lax.rem(place + 1, parts)
    lower = lax.rem(place + parts - 1, parts)

    barrier = pltpu.get_barrier_semaphore()
    for step in range(1, groups):
        pl.semaphore_signal(barrier, inc=1, device_id={"inst": lax.rem(me + step, groups)}, device_id_type=MESH)
    for other in (upper, lower):
        pl.semaphore_signal(barrier, inc=1, device_id={"mesh": other}, device_id_type=MESH)

    fetches = [
        pltpu.make_async_copy(source, target, local_sem.at[i])
        for i, (source, target) in enumerate(
            [(state_hbm, own), (list_hbm, listed), (count_hbm, counts), (slot_hbm, slots), (index_hbm, index), (cell_hbm, cell)]
        )
    ]
    for fetch in fetches:
        fetch.start()
    face_fetches = [
        pltpu.make_async_copy(face_hbm.at[n, k], face.at[n, k], face_sem.at[n * nb + k])
        for n in range(inst) for k in range(nb)
    ]
    for fetch in face_fetches:
        fetch.start()

    fetches[0].wait()
    for j in range(groups):
        for a in range(nvar):
            pieces = [own[n, a, j * share:(j + 1) * share, :] for n in range(inst)]
            outgoing[j, a, 0:rows, :] = jnp.concatenate(pieces, axis=0) if inst > 1 else pieces[0]
    pl.semaphore_wait(barrier, groups + 1)

    first = []
    for step in range(1, groups):
        target = lax.rem(me + step, groups)
        copy = pltpu.make_async_remote_copy(
            src_ref=outgoing.at[target], dst_ref=incoming.at[step],
            send_sem=send_one.at[step], recv_sem=recv_one.at[step],
            device_id={"inst": target}, device_id_type=MESH,
        )
        copy.start()
        first.append(copy)
    incoming[0] = outgoing[me]

    for n in range(inst):
        for b in range(nvar):
            column = (n * nvar + b) * LANES
            for i, piece in enumerate(split(own[n, b])):
                table[i * tiles:(i + 1) * tiles, column:column + LANES] = piece
    fetches[1].wait()
    fetches[2].wait()
    lane = lax.broadcasted_iota(jnp.int32, (most, 3 * tiles), 1) % tiles
    row = lax.broadcasted_iota(jnp.int32, (most, 3 * tiles), 0)
    wanted = listed[...].T
    picks = []
    for d in range(2):
        chosen = (lane == wanted[:, d:d + 1]) & (row < counts[0:1, d:d + 1])
        picks.append(jnp.where(chosen, 1.0, 0.0))
    pick = jnp.concatenate(picks, axis=0).astype(jnp.bfloat16)
    picked = jnp.dot(pick, table[0:3 * tiles, :], preferred_element_type=jnp.float32)
    for d in range(2):
        for n in range(inst):
            for b in range(nvar):
                column = (n * nvar + b) * LANES
                packets[d, n, b] = picked[d * most:(d + 1) * most, column:column + LANES]
    halos = []
    for d, other in ((1, upper), (0, lower)):
        copy = pltpu.make_async_remote_copy(
            src_ref=packets.at[d], dst_ref=halo.at[1 - d],
            send_sem=send_halo.at[d], recv_sem=recv_halo.at[1 - d],
            device_id={"mesh": other}, device_id_type=MESH,
        )
        copy.start()
        halos.append(copy)

    fetches[3].wait()
    width = 3 * (tiles + 2 * most)
    lane = lax.broadcasted_iota(jnp.int32, (tiles, width), 1)
    lane = jnp.where(lane < 3 * tiles, lane % tiles, tiles + (lane - 3 * tiles) % (2 * most))
    slot = slots[...].T
    chooser = jnp.concatenate(
        [jnp.where(lane == slot[:, k:k + 1], 1.0, 0.0).astype(jnp.bfloat16) for k in range(nb)], axis=0
    )

    fetches[5].wait()
    for start in range(0, tiles, ROWS):
        part = slice(start, start + ROWS)
        for n in range(inst):
            values = [own[n, b, part, :] for b in range(nvar)]
            for a in range(nvar):
                term = cell[n, a, 0, part, :] * values[0]
                for b in range(1, nvar):
                    term += cell[n, a, b, part, :] * values[b]
                total[n, a, part, :] = term

    place_row = lax.broadcasted_iota(jnp.int32, (rows, LANES), 0)
    weights = {}

    def weight(distance, shift):
        key = (distance % groups, shift)
        if key not in weights:
            values = [
                spectral_coefficient(distance * inst + i - (i + shift) % inst, count) for i in range(inst)
            ]
            made = jnp.full((rows, LANES), values[-1], jnp.float32)
            for i in range(inst - 2, -1, -1):
                made = jnp.where(place_row < (i + 1) * share, values[i], made)
            weights[key] = made
        return weights[key]

    for copy in first:
        copy.wait_recv()
    for a in range(nvar):
        sources = []
        for step in range(groups):
            value = incoming[step, a, 0:rows, :]
            turned = [value]
            for shift in range(1, inst):
                turned.append(jnp.concatenate([value[shift * share:], value[:shift * share]], axis=0))
            sources.append(turned)
        for ahead in range(groups):
            sums = None
            for step in range(groups):
                for shift in range(inst):
                    term = weight(ahead + step, shift) * sources[step][shift]
                    sums = term if sums is None else sums + term
            solved[ahead, a, 0:rows, :] = sums
    second = []
    for ahead in range(1, groups):
        target = lax.rem(me + ahead, groups)
        copy = pltpu.make_async_remote_copy(
            src_ref=solved.at[ahead], dst_ref=returned.at[me],
            send_sem=send_two.at[ahead], recv_sem=recv_two.at[ahead],
            device_id={"inst": target}, device_id_type=MESH,
        )
        copy.start()
        second.append(copy)
    returned[me] = solved[0]

    for copy in halos:
        copy.wait_recv()
    for n in range(inst):
        for b in range(nvar):
            column = (n * nvar + b) * LANES
            both = jnp.concatenate([halo[0, n, b], halo[1, n, b]], axis=0)
            for i, piece in enumerate(split(both)):
                top = 3 * tiles + i * 2 * most
                table[top:top + 2 * most, column:column + LANES] = piece
    facing[...] = jnp.dot(chooser, table[...], preferred_element_type=jnp.float32)
    fetches[4].wait()
    for fetch in face_fetches:
        fetch.wait()

    def octet(o, carry):
        part = pl.ds(pl.multiple_of(o * ROWS, ROWS), ROWS)
        for n in range(inst):
            sums = [total[n, a, part, :] for a in range(nvar)]
            for k in range(nb):
                cells = index[k, part, :]
                where = pl.ds(pl.multiple_of(k * tiles + o * ROWS, ROWS), ROWS)
                for b in range(nvar):
                    column = (n * nvar + b) * LANES
                    value = jnp.take_along_axis(
                        facing[where, column:column + LANES], cells, axis=1, mode="promise_in_bounds"
                    )
                    for a in range(nvar):
                        sums[a] += face[n, k, a, b, part, :] * value
            for a in range(nvar):
                total[n, a, part, :] = sums[a]
        return carry

    lax.fori_loop(0, tiles // ROWS, octet, 0)

    for copy in second:
        copy.wait_recv()
    each = ROWS // share
    for n in range(inst):
        for a in range(nvar):
            for o in range(tiles // ROWS):
                pieces = [returned[o * each + i, a, n * share:(n + 1) * share, :] for i in range(each)]
                part = slice(o * ROWS, (o + 1) * ROWS)
                out_ref[n, a, part, :] = total[n, a, part, :] + jnp.concatenate(pieces, axis=0)
    for copy in first + halos + second:
        copy.wait_send()


def shards(groups, parts, state, cell_block, face_block, neighbor, face_cell, send_list, send_count):
    inst, tiles, nvar, lanes = state.shape
    nb = neighbor.shape[1]
    most = send_list.shape[2]
    operands = (
        jnp.transpose(state, (0, 2, 1, 3)),
        jnp.transpose(cell_block, (0, 2, 3, 1, 4)),
        jnp.transpose(face_block, (0, 2, 3, 4, 1, 5)),
        jnp.transpose(neighbor),
        jnp.transpose(face_cell, (1, 0, 2)),
        send_list[0],
        send_count,
    )
    packed = (groups, nvar, ROWS, lanes)
    dma = pltpu.SemaphoreType.DMA
    scratch = [pltpu.VMEM(x.shape, x.dtype) for x in operands] + [
        pltpu.VMEM(packed, jnp.float32),
        pltpu.VMEM(packed, jnp.float32),
        pltpu.VMEM(packed, jnp.float32),
        pltpu.VMEM(packed, jnp.float32),
        pltpu.VMEM((2, inst, nvar, most, lanes), jnp.float32),
        pltpu.VMEM((2, inst, nvar, most, lanes), jnp.float32),
        pltpu.VMEM((3 * (tiles + 2 * most), inst * nvar * lanes), jnp.bfloat16),
        pltpu.VMEM((nb * tiles, inst * nvar * lanes), jnp.float32),
        pltpu.VMEM((inst, nvar, tiles, lanes), jnp.float32),
        dma((6,)), dma((inst * nb,)),
        dma((groups,)), dma((groups,)), dma((groups,)), dma((groups,)),
        dma((2,)), dma((2,)),
    ]
    product = pl.pallas_call(
        functools.partial(kernel, groups, parts),
        out_shape=jax.ShapeDtypeStruct((inst, nvar, tiles, lanes), jnp.float32),
        in_specs=[pl.BlockSpec(memory_space=pl.ANY)] * len(operands),
        out_specs=pl.BlockSpec(memory_space=pltpu.VMEM),
        scratch_shapes=scratch,
        compiler_params=pltpu.CompilerParams(
            collective_id=0, has_side_effects=True, vmem_limit_bytes=56 * 1024 * 1024
        ),
    )(*operands)
    return jnp.transpose(product, (0, 2, 1, 3))


def solution(mesh):
    placed = (
        P("inst", "mesh", None, None),
        P("inst", "mesh", None, None, None),
        P("inst", "mesh", None, None, None, None),
        P("mesh", None),
        P("mesh", None, None),
        P("mesh", None, None),
        P("mesh", None),
    )
    return jax.shard_map(
        functools.partial(shards, mesh.shape["inst"], mesh.shape["mesh"]),
        mesh=mesh, in_specs=placed, out_specs=P("inst", "mesh", None, None), check_vma=False,
    )
```

```python
import functools
import math

import jax
import jax.numpy as jnp
from jax import lax
from jax.experimental import pallas as pl
from jax.experimental.pallas import tpu as pltpu
from jax.sharding import PartitionSpec as P

DISSIPATION = 0.05
LANES = 128
ROWS = 8
MESH = pl.DeviceIdType.MESH


def spectral_coefficient(offset, count):
    offset = offset % count
    if offset == 0:
        return -DISSIPATION * (count * count + 2) / 12.0
    angle = math.pi * offset / count
    parity = 1 - 2 * (offset % 2)
    sine = math.sin(angle)
    return 0.5 * parity * math.cos(angle) / sine - DISSIPATION * 0.5 * parity / (sine * sine)


def split(values):
    high = values.astype(jnp.bfloat16)
    rest = values - high.astype(jnp.float32)
    middle = rest.astype(jnp.bfloat16)
    low = (rest - middle.astype(jnp.float32)).astype(jnp.bfloat16)
    return high, middle, low


def kernel(
    groups, parts,
    state_hbm, cell_hbm, face_hbm, slot_hbm, index_hbm, list_hbm, count_hbm,
    out_ref,
    own, cell, face, slots, index, listed, counts,
    outgoing, incoming, solved, returned, packets, halo, table, facing, total,
    local_sem, face_sem, send_one, recv_one, send_two, recv_two, send_halo, recv_halo,
):
    inst, nvar, tiles = own.shape[0], own.shape[1], own.shape[2]
    nb = index.shape[0]
    most = listed.shape[1]
    share = tiles // groups
    count = inst * groups
    rows = inst * share
    me = lax.axis_index("inst")
    place = lax.axis_index("mesh")
    upper = lax.rem(place + 1, parts)
    lower = lax.rem(place + parts - 1, parts)

    barrier = pltpu.get_barrier_semaphore()
    for step in range(1, groups):
        pl.semaphore_signal(barrier, inc=1, device_id={"inst": lax.rem(me + step, groups)}, device_id_type=MESH)
    for other in (upper, lower):
        pl.semaphore_signal(barrier, inc=1, device_id={"mesh": other}, device_id_type=MESH)

    fetches = [
        pltpu.make_async_copy(source, target, local_sem.at[i])
        for i, (source, target) in enumerate(
            [(state_hbm, own), (list_hbm, listed), (count_hbm, counts), (slot_hbm, slots), (index_hbm, index), (cell_hbm, cell)]
        )
    ]
    for fetch in fetches:
        fetch.start()
    face_fetches = [
        pltpu.make_async_copy(face_hbm.at[n, k], face.at[n, k], face_sem.at[n * nb + k])
        for n in range(inst) for k in range(nb)
    ]
    for fetch in face_fetches:
        fetch.start()

    fetches[0].wait()
    for j in range(groups):
        for a in range(nvar):
            pieces = [own[n, a, j * share:(j + 1) * share, :] for n in range(inst)]
            outgoing[j, a, 0:rows, :] = jnp.concatenate(pieces, axis=0) if inst > 1 else pieces[0]
    pl.semaphore_wait(barrier, groups + 1)

    first = []
    for step in range(1, groups):
        target = lax.rem(me + step, groups)
        copy = pltpu.make_async_remote_copy(
            src_ref=outgoing.at[target], dst_ref=incoming.at[step],
            send_sem=send_one.at[step], recv_sem=recv_one.at[step],
            device_id={"inst": target}, device_id_type=MESH,
        )
        copy.start()
        first.append(copy)
    incoming[0] = outgoing[me]

    for n in range(inst):
        for b in range(nvar):
            column = (n * nvar + b) * LANES
            for i, piece in enumerate(split(own[n, b])):
                table[i * tiles:(i + 1) * tiles, column:column + LANES] = piece
    fetches[1].wait()
    fetches[2].wait()
    lane = lax.broadcasted_iota(jnp.int32, (most, 3 * tiles), 1) % tiles
    row = lax.broadcasted_iota(jnp.int32, (most, 3 * tiles), 0)
    wanted = listed[...].T
    picks = []
    for d in range(2):
        chosen = (lane == wanted[:, d:d + 1]) & (row < counts[0:1, d:d + 1])
        picks.append(jnp.where(chosen, 1.0, 0.0))
    pick = jnp.concatenate(picks, axis=0).astype(jnp.bfloat16)
    picked = jnp.dot(pick, table[0:3 * tiles, :], preferred_element_type=jnp.float32)
    for d in range(2):
        for n in range(inst):
            for b in range(nvar):
                column = (n * nvar + b) * LANES
                packets[d, n, b] = picked[d * most:(d + 1) * most, column:column + LANES]
    halos = []
    for d, other in ((1, upper), (0, lower)):
        copy = pltpu.make_async_remote_copy(
            src_ref=packets.at[d], dst_ref=halo.at[1 - d],
            send_sem=send_halo.at[d], recv_sem=recv_halo.at[1 - d],
            device_id={"mesh": other}, device_id_type=MESH,
        )
        copy.start()
        halos.append(copy)

    fetches[3].wait()
    width = 3 * (tiles + 2 * most)
    lane = lax.broadcasted_iota(jnp.int32, (tiles, width), 1)
    lane = jnp.where(lane < 3 * tiles, lane % tiles, tiles + (lane - 3 * tiles) % (2 * most))
    slot = slots[...].T
    chooser = jnp.concatenate(
        [jnp.where(lane == slot[:, k:k + 1], 1.0, 0.0).astype(jnp.bfloat16) for k in range(nb)], axis=0
    )

    fetches[5].wait()
    for start in range(0, tiles, ROWS):
        part = slice(start, start + ROWS)
        for n in range(inst):
            values = [own[n, b, part, :] for b in range(nvar)]
            for a in range(nvar):
                term = cell[n, a, 0, part, :] * values[0]
                for b in range(1, nvar):
                    term += cell[n, a, b, part, :] * values[b]
                total[n, a, part, :] = term

    place_row = lax.broadcasted_iota(jnp.int32, (rows, LANES), 0)
    weights = {}

    def weight(distance, shift):
        key = (distance % groups, shift)
        if key not in weights:
            values = [
                spectral_coefficient(distance * inst + i - (i + shift) % inst, count) for i in range(inst)
            ]
            made = jnp.full((rows, LANES), values[-1], jnp.float32)
            for i in range(inst - 2, -1, -1):
                made = jnp.where(place_row < (i + 1) * share, values[i], made)
            weights[key] = made
        return weights[key]

    for copy in first:
        copy.wait_recv()
    for a in range(nvar):
        sources = []
        for step in range(groups):
            value = incoming[step, a, 0:rows, :]
            turned = [value]
            for shift in range(1, inst):
                turned.append(jnp.concatenate([value[shift * share:], value[:shift * share]], axis=0))
            sources.append(turned)
        for ahead in range(groups):
            sums = None
            for step in range(groups):
                for shift in range(inst):
                    term = weight(ahead + step, shift) * sources[step][shift]
                    sums = term if sums is None else sums + term
            solved[ahead, a, 0:rows, :] = sums
    second = []
    for ahead in range(1, groups):
        target = lax.rem(me + ahead, groups)
        copy = pltpu.make_async_remote_copy(
            src_ref=solved.at[ahead], dst_ref=returned.at[me],
            send_sem=send_two.at[ahead], recv_sem=recv_two.at[ahead],
            device_id={"inst": target}, device_id_type=MESH,
        )
        copy.start()
        second.append(copy)
    returned[me] = solved[0]

    for copy in halos:
        copy.wait_recv()
    for n in range(inst):
        for b in range(nvar):
            column = (n * nvar + b) * LANES
            both = jnp.concatenate([halo[0, n, b], halo[1, n, b]], axis=0)
            for i, piece in enumerate(split(both)):
                top = 3 * tiles + i * 2 * most
                table[top:top + 2 * most, column:column + LANES] = piece
    facing[...] = jnp.dot(chooser, table[...], preferred_element_type=jnp.float32)
    fetches[4].wait()
    for fetch in face_fetches:
        fetch.wait()

    def octet(o, carry):
        part = pl.ds(pl.multiple_of(o * ROWS, ROWS), ROWS)
        for n in range(inst):
            sums = [total[n, a, part, :] for a in range(nvar)]
            for k in range(nb):
                cells = index[k, part, :]
                where = pl.ds(pl.multiple_of(k * tiles + o * ROWS, ROWS), ROWS)
                for b in range(nvar):
                    column = (n * nvar + b) * LANES
                    value = jnp.take_along_axis(
                        facing[where, column:column + LANES], cells, axis=1, mode="promise_in_bounds"
                    )
                    for a in range(nvar):
                        sums[a] += face[n, k, a, b, part, :] * value
            for a in range(nvar):
                total[n, a, part, :] = sums[a]
        return carry

    lax.fori_loop(0, tiles // ROWS, octet, 0)

    for copy in second:
        copy.wait_recv()
    each = ROWS // share
    for n in range(inst):
        for a in range(nvar):
            for o in range(tiles // ROWS):
                pieces = [returned[o * each + i, a, n * share:(n + 1) * share, :] for i in range(each)]
                part = slice(o * ROWS, (o + 1) * ROWS)
                out_ref[n, a, part, :] = total[n, a, part, :] + jnp.concatenate(pieces, axis=0)
    for copy in first + halos + second:
        copy.wait_send()


def shards(groups, parts, state, cell_block, face_block, neighbor, face_cell, send_list, send_count):
    inst, tiles, nvar, lanes = state.shape
    nb = neighbor.shape[1]
    most = send_list.shape[2]
    operands = (
        jnp.transpose(state, (0, 2, 1, 3)),
        jnp.transpose(cell_block, (0, 2, 3, 1, 4)),
        jnp.transpose(face_block, (0, 2, 3, 4, 1, 5)),
        jnp.transpose(neighbor),
        jnp.transpose(face_cell, (1, 0, 2)),
        send_list[0],
        send_count,
    )
    packed = (groups, nvar, ROWS, lanes)
    dma = pltpu.SemaphoreType.DMA
    scratch = [pltpu.VMEM(x.shape, x.dtype) for x in operands] + [
        pltpu.VMEM(packed, jnp.float32),
        pltpu.VMEM(packed, jnp.float32),
        pltpu.VMEM(packed, jnp.float32),
        pltpu.VMEM(packed, jnp.float32),
        pltpu.VMEM((2, inst, nvar, most, lanes), jnp.float32),
        pltpu.VMEM((2, inst, nvar, most, lanes), jnp.float32),
        pltpu.VMEM((3 * (tiles + 2 * most), inst * nvar * lanes), jnp.bfloat16),
        pltpu.VMEM((nb * tiles, inst * nvar * lanes), jnp.float32),
        pltpu.VMEM((inst, nvar, tiles, lanes), jnp.float32),
        dma((6,)), dma((inst * nb,)),
        dma((groups,)), dma((groups,)), dma((groups,)), dma((groups,)),
        dma((2,)), dma((2,)),
    ]
    product = pl.pallas_call(
        functools.partial(kernel, groups, parts),
        out_shape=pltpu.VMEM((inst, nvar, tiles, lanes), jnp.float32),
        in_specs=[pl.BlockSpec(memory_space=pl.ANY)] * len(operands),
        out_specs=pl.BlockSpec(memory_space=pltpu.VMEM),
        scratch_shapes=scratch,
        compiler_params=pltpu.CompilerParams(
            collective_id=0, has_side_effects=True, vmem_limit_bytes=56 * 1024 * 1024
        ),
    )(*operands)
    return jnp.transpose(product, (0, 2, 1, 3))


def solution(mesh):
    placed = (
        P("inst", "mesh", None, None),
        P("inst", "mesh", None, None, None),
        P("inst", "mesh", None, None, None, None),
        P("mesh", None),
        P("mesh", None, None),
        P("mesh", None, None),
        P("mesh", None),
    )
    return jax.shard_map(
        functools.partial(shards, mesh.shape["inst"], mesh.shape["mesh"]),
        mesh=mesh, in_specs=placed, out_specs=P("inst", "mesh", None, None), check_vma=False,
    )
```

```python
import functools
import math

import jax
import jax.numpy as jnp
from jax import lax
from jax.experimental import pallas as pl
from jax.experimental.pallas import tpu as pltpu
from jax.sharding import PartitionSpec as P

DISSIPATION = 0.05
LANES = 128
ROWS = 8
MESH = pl.DeviceIdType.MESH


def spectral_coefficient(offset, count):
    offset = offset % count
    if offset == 0:
        return -DISSIPATION * (count * count + 2) / 12.0
    angle = math.pi * offset / count
    parity = 1 - 2 * (offset % 2)
    sine = math.sin(angle)
    return 0.5 * parity * math.cos(angle) / sine - DISSIPATION * 0.5 * parity / (sine * sine)


def split(values):
    high = values.astype(jnp.bfloat16)
    rest = values - high.astype(jnp.float32)
    middle = rest.astype(jnp.bfloat16)
    low = (rest - middle.astype(jnp.float32)).astype(jnp.bfloat16)
    return high, middle, low


def kernel(
    groups, parts,
    state_hbm, cell_hbm, face_hbm, slot_hbm, index_hbm, list_hbm, count_hbm,
    out_ref,
    own, cell, face, slots, index, listed, counts,
    outgoing, incoming, solved, returned, packets, halo, table, facing, total,
    local_sem, face_sem, send_one, recv_one, send_two, recv_two, send_halo, recv_halo,
):
    inst, nvar, tiles = own.shape[0], own.shape[1], own.shape[2]
    nb = index.shape[0]
    most = listed.shape[1]
    share = tiles // groups
    count = inst * groups
    rows = inst * share
    me = lax.axis_index("inst")
    place = lax.axis_index("mesh")
    upper = lax.rem(place + 1, parts)
    lower = lax.rem(place + parts - 1, parts)

    barrier = pltpu.get_barrier_semaphore()
    for step in range(1, groups):
        pl.semaphore_signal(barrier, inc=1, device_id={"inst": lax.rem(me + step, groups)}, device_id_type=MESH)
    for other in (upper, lower):
        pl.semaphore_signal(barrier, inc=1, device_id={"mesh": other}, device_id_type=MESH)

    fetches = [
        pltpu.make_async_copy(source, target, local_sem.at[i])
        for i, (source, target) in enumerate(
            [(state_hbm, own), (list_hbm, listed), (count_hbm, counts), (slot_hbm, slots), (index_hbm, index), (cell_hbm, cell)]
        )
    ]
    for fetch in fetches:
        fetch.start()
    face_fetches = [
        pltpu.make_async_copy(face_hbm.at[n, k], face.at[n, k], face_sem.at[n * nb + k])
        for n in range(inst) for k in range(nb)
    ]
    for fetch in face_fetches:
        fetch.start()

    fetches[0].wait()
    for j in range(groups):
        for a in range(nvar):
            pieces = [own[n, a, j * share:(j + 1) * share, :] for n in range(inst)]
            outgoing[j, a, 0:rows, :] = jnp.concatenate(pieces, axis=0) if inst > 1 else pieces[0]
    pl.semaphore_wait(barrier, groups + 1)

    cuts = ((0, 2), (2, nvar))
    first = []
    for c, (low, high) in enumerate(cuts):
        for step in range(1, groups):
            target = lax.rem(me + step, groups)
            copy = pltpu.make_async_remote_copy(
                src_ref=outgoing.at[target, low:high], dst_ref=incoming.at[step, low:high],
                send_sem=send_one.at[c, step], recv_sem=recv_one.at[c, step],
                device_id={"inst": target}, device_id_type=MESH,
            )
            copy.start()
            first.append(copy)
    incoming[0] = outgoing[me]

    for n in range(inst):
        for b in range(nvar):
            column = (n * nvar + b) * LANES
            for i, piece in enumerate(split(own[n, b])):
                table[i * tiles:(i + 1) * tiles, column:column + LANES] = piece
    fetches[1].wait()
    fetches[2].wait()
    lane = lax.broadcasted_iota(jnp.int32, (most, 3 * tiles), 1) % tiles
    row = lax.broadcasted_iota(jnp.int32, (most, 3 * tiles), 0)
    wanted = listed[...].T
    picks = []
    for d in range(2):
        chosen = (lane == wanted[:, d:d + 1]) & (row < counts[0:1, d:d + 1])
        picks.append(jnp.where(chosen, 1.0, 0.0))
    pick = jnp.concatenate(picks, axis=0).astype(jnp.bfloat16)
    picked = jnp.dot(pick, table[0:3 * tiles, :], preferred_element_type=jnp.float32)
    for d in range(2):
        for n in range(inst):
            for b in range(nvar):
                column = (n * nvar + b) * LANES
                packets[d, n, b] = picked[d * most:(d + 1) * most, column:column + LANES]
    halos = []
    for d, other in ((1, upper), (0, lower)):
        copy = pltpu.make_async_remote_copy(
            src_ref=packets.at[d], dst_ref=halo.at[1 - d],
            send_sem=send_halo.at[d], recv_sem=recv_halo.at[1 - d],
            device_id={"mesh": other}, device_id_type=MESH,
        )
        copy.start()
        halos.append(copy)

    fetches[3].wait()
    width = 3 * (tiles + 2 * most)
    lane = lax.broadcasted_iota(jnp.int32, (tiles, width), 1)
    lane = jnp.where(lane < 3 * tiles, lane % tiles, tiles + (lane - 3 * tiles) % (2 * most))
    slot = slots[...].T
    chooser = jnp.concatenate(
        [jnp.where(lane == slot[:, k:k + 1], 1.0, 0.0).astype(jnp.bfloat16) for k in range(nb)], axis=0
    )

    fetches[5].wait()
    for start in range(0, tiles, ROWS):
        part = slice(start, start + ROWS)
        for n in range(inst):
            values = [own[n, b, part, :] for b in range(nvar)]
            for a in range(nvar):
                term = cell[n, a, 0, part, :] * values[0]
                for b in range(1, nvar):
                    term += cell[n, a, b, part, :] * values[b]
                total[n, a, part, :] = term

    place_row = lax.broadcasted_iota(jnp.int32, (rows, LANES), 0)
    weights = {}

    half = groups // 2

    def weight(distance, shift, sign):
        key = (distance % groups, shift, sign)
        if key not in weights:
            offsets = [distance * inst + i - (i + shift) % inst for i in range(inst)]
            values = [
                0.5 * (spectral_coefficient(x, count) + sign * spectral_coefficient(x + count // 2, count))
                for x in offsets
            ]
            made = jnp.full((rows, LANES), values[-1], jnp.float32)
            for i in range(inst - 2, -1, -1):
                made = jnp.where(place_row < (i + 1) * share, values[i], made)
            weights[key] = made
        return weights[key]

    second = []
    for c, (low, high) in enumerate(cuts):
        for copy in first[c * (groups - 1):(c + 1) * (groups - 1)]:
            copy.wait_recv()
        for a in range(low, high):
            sources = []
            for step in range(groups):
                value = incoming[step, a, 0:rows, :]
                turned = [value]
                for shift in range(1, inst):
                    turned.append(jnp.concatenate([value[shift * share:], value[:shift * share]], axis=0))
                sources.append(turned)
            sums = [[x + y for x, y in zip(sources[i], sources[i + half])] for i in range(half)]
            differences = [[x - y for x, y in zip(sources[i], sources[i + half])] for i in range(half)]
            for ahead in range(half):
                even = odd = None
                for step in range(half):
                    for shift in range(inst):
                        plus = weight(ahead + step, shift, 1.0) * sums[step][shift]
                        minus = weight(ahead + step, shift, -1.0) * differences[step][shift]
                        even = plus if even is None else even + plus
                        odd = minus if odd is None else odd + minus
                solved[ahead, a, 0:rows, :] = even + odd
                solved[ahead + half, a, 0:rows, :] = even - odd
        for ahead in range(1, groups):
            target = lax.rem(me + ahead, groups)
            copy = pltpu.make_async_remote_copy(
                src_ref=solved.at[ahead, low:high], dst_ref=returned.at[me, low:high],
                send_sem=send_two.at[c, ahead], recv_sem=recv_two.at[c, ahead],
                device_id={"inst": target}, device_id_type=MESH,
            )
            copy.start()
            second.append(copy)
    returned[me] = solved[0]

    for copy in halos:
        copy.wait_recv()
    for n in range(inst):
        for b in range(nvar):
            column = (n * nvar + b) * LANES
            both = jnp.concatenate([halo[0, n, b], halo[1, n, b]], axis=0)
            for i, piece in enumerate(split(both)):
                top = 3 * tiles + i * 2 * most
                table[top:top + 2 * most, column:column + LANES] = piece
    facing[...] = jnp.dot(chooser, table[...], preferred_element_type=jnp.float32)
    fetches[4].wait()
    for fetch in face_fetches:
        fetch.wait()

    def octet(o, carry):
        part = pl.ds(pl.multiple_of(o * ROWS, ROWS), ROWS)
        for n in range(inst):
            sums = [total[n, a, part, :] for a in range(nvar)]
            for k in range(nb):
                cells = index[k, part, :]
                where = pl.ds(pl.multiple_of(k * tiles + o * ROWS, ROWS), ROWS)
                for b in range(nvar):
                    column = (n * nvar + b) * LANES
                    value = jnp.take_along_axis(
                        facing[where, column:column + LANES], cells, axis=1, mode="promise_in_bounds"
                    )
                    for a in range(nvar):
                        sums[a] += face[n, k, a, b, part, :] * value
            for a in range(nvar):
                total[n, a, part, :] = sums[a]
        return carry

    lax.fori_loop(0, tiles // ROWS, octet, 0)

    for copy in second:
        copy.wait_recv()
    each = ROWS // share
    for n in range(inst):
        for a in range(nvar):
            for o in range(tiles // ROWS):
                pieces = [returned[o * each + i, a, n * share:(n + 1) * share, :] for i in range(each)]
                part = slice(o * ROWS, (o + 1) * ROWS)
                out_ref[n, a, part, :] = total[n, a, part, :] + jnp.concatenate(pieces, axis=0)
    for copy in first + halos + second:
        copy.wait_send()


def shards(groups, parts, state, cell_block, face_block, neighbor, face_cell, send_list, send_count):
    inst, tiles, nvar, lanes = state.shape
    nb = neighbor.shape[1]
    most = send_list.shape[2]
    operands = (
        jnp.transpose(state, (0, 2, 1, 3)),
        jnp.transpose(cell_block, (0, 2, 3, 1, 4)),
        jnp.transpose(face_block, (0, 2, 3, 4, 1, 5)),
        jnp.transpose(neighbor),
        jnp.transpose(face_cell, (1, 0, 2)),
        send_list[0],
        send_count,
    )
    packed = (groups, nvar, ROWS, lanes)
    dma = pltpu.SemaphoreType.DMA
    scratch = [pltpu.VMEM(x.shape, x.dtype) for x in operands] + [
        pltpu.VMEM(packed, jnp.float32),
        pltpu.VMEM(packed, jnp.float32),
        pltpu.VMEM(packed, jnp.float32),
        pltpu.VMEM(packed, jnp.float32),
        pltpu.VMEM((2, inst, nvar, most, lanes), jnp.float32),
        pltpu.VMEM((2, inst, nvar, most, lanes), jnp.float32),
        pltpu.VMEM((3 * (tiles + 2 * most), inst * nvar * lanes), jnp.bfloat16),
        pltpu.VMEM((nb * tiles, inst * nvar * lanes), jnp.float32),
        pltpu.VMEM((inst, nvar, tiles, lanes), jnp.float32),
        dma((6,)), dma((inst * nb,)),
        dma((2, groups)), dma((2, groups)), dma((2, groups)), dma((2, groups)),
        dma((2,)), dma((2,)),
    ]
    product = pl.pallas_call(
        functools.partial(kernel, groups, parts),
        out_shape=pltpu.VMEM((inst, nvar, tiles, lanes), jnp.float32),
        in_specs=[pl.BlockSpec(memory_space=pl.ANY)] * len(operands),
        out_specs=pl.BlockSpec(memory_space=pltpu.VMEM),
        scratch_shapes=scratch,
        compiler_params=pltpu.CompilerParams(
            collective_id=0, has_side_effects=True, vmem_limit_bytes=56 * 1024 * 1024
        ),
    )(*operands)
    return jnp.transpose(product, (0, 2, 1, 3))


def solution(mesh):
    placed = (
        P("inst", "mesh", None, None),
        P("inst", "mesh", None, None, None),
        P("inst", "mesh", None, None, None, None),
        P("mesh", None),
        P("mesh", None, None),
        P("mesh", None, None),
        P("mesh", None),
    )
    return jax.shard_map(
        functools.partial(shards, mesh.shape["inst"], mesh.shape["mesh"]),
        mesh=mesh, in_specs=placed, out_specs=P("inst", "mesh", None, None), check_vma=False,
    )
```
